256 devices in a mesh: focus: 8 (over x_hi, y), band: 32 (over z, x_lo, core).
Axes of the slice: x: 4 (x_hi: 2, x_lo: 2; x = x_hi * 2 + x_lo), y: 4, z: 8, core: 2. Of those that a mesh axis runs over, the one named last changes fastest.
Arguments:
- planes: bfloat16 [24, 768, 16384], P('focus', 'band'), may hold values from 0.05 to 3.5
- focus_z: float32 [24], replicated, may hold values from -1.25 to 1.25, as said below
Outputs:
- phase: float32 [768, 16384], P('band', 'focus')
- residual: float32 [768, 16384], P('band', 'focus')
The draws below stay inside these ranges and needn't reach their ends.
Inputs may be any that keep to these rules, and one draw needn't show every extreme that they name: `focus_z`: strictly increasing; consecutive positions differ by 0.01 or more.
All inputs are finite; a program needn't handle non-finite values.
Results may differ from the reference program's by a relative error of at most 0.00075.
Values may be sent and summed in bfloat16 or wider, within the bound.
No kernel may reach another device: no remote copies, remote signals or barrier semaphores. Data moves between devices by JAX's collectives and lax.ppermute only.
A program may use at most 64 MiB of HBM per device.

```python
import math
import jax
import jax.numpy as jnp
from jax import lax

ITERS = 3
PLANES = 24
ROWS = 768
COLS = 16384


def draw_planes(key, part):
    key = jax.random.fold_in(key, 11)
    base_key, rough_key = jax.random.split(key)
    base = jnp.exp(jax.random.uniform(base_key, (ROWS, COLS), jnp.float32, math.log(0.5), math.log(2.0)))
    rough = jax.random.uniform(rough_key, (PLANES, ROWS, COLS), jnp.float32, -1.0, 1.0)
    row_frac = jnp.arange(ROWS, dtype=jnp.float32) / max(ROWS - 1, 1)
    col_frac = jnp.arange(COLS, dtype=jnp.float32) / max(COLS - 1, 1)
    amp = 0.06 * (3.0 ** row_frac)[:, None] * (3.0 ** col_frac)[None, :]
    noise = rough
    return (base[None] * (1.0 + amp[None] * noise)).astype(jnp.bfloat16)


def draw_focus_z(key, part):
    key = jax.random.fold_in(key, 23)
    jitter = jax.random.uniform(key, (PLANES,), jnp.float32, -0.3, 0.3)
    centre = jnp.arange(PLANES, dtype=jnp.float32) - 0.5 * (PLANES - 1)
    return 0.1 * (centre + jitter)


def setup_inputs(seed: int = 0) -> dict:
    streams_of = jax.random.split(jax.random.key(seed), 3)
    return {
        "planes": draw_planes(jax.random.fold_in(streams_of[2], 71), 0),
        "focus_z": draw_focus_z(jax.random.fold_in(streams_of[2], 71), 0),
    }


def slope_weights(focus_z):
    offset = focus_z - jnp.mean(focus_z)
    return offset / jnp.sum(offset * offset)


def face_terms(intensity):
    padded = jnp.pad(intensity, 1)
    north = 0.5 * (intensity + padded[:-2, 1:-1])
    south = 0.5 * (intensity + padded[2:, 1:-1])
    west = 0.5 * (intensity + padded[1:-1, :-2])
    east = 0.5 * (intensity + padded[1:-1, 2:])
    return north + south + west + east, north, south, west, east


def operate(field, terms):
    diag, north, south, west, east = terms
    padded = jnp.pad(field, 1)
    beside = north * padded[:-2, 1:-1] + south * padded[2:, 1:-1]
    beside = beside + west * padded[1:-1, :-2] + east * padded[1:-1, 2:]
    return diag * field - beside


def reference(planes, focus_z):
    weights = slope_weights(focus_z)

    def accumulate(carry, item):
        weight, plane = item
        value = plane.astype(jnp.float32)
        return (carry[0] + weight * value, carry[1] + value), None

    start = jnp.zeros((ROWS, COLS), jnp.float32)
    (slope, total), unused = lax.scan(accumulate, (start, start), (weights, planes))
    intensity = total / PLANES
    rhs = 20.0 * slope
    terms = face_terms(intensity)
    diag = terms[0]
    phase = jnp.zeros_like(rhs)
    residual = rhs
    pre = residual / diag
    direction = pre
    rz_now = jnp.sum(residual * pre)
    for step in range(ITERS):
        image = operate(direction, terms)
        alpha = rz_now / jnp.sum(direction * image)
        phase = phase + alpha * direction
        residual = residual - alpha * image
        pre = residual / diag
        rz_next = jnp.sum(residual * pre)
        direction = pre + (rz_next / rz_now) * direction
        rz_now = rz_next
    return phase, residual
```

```python
import functools

import jax
import jax.numpy as jnp
import numpy as np
from jax import lax
from jax.experimental import pallas as pl
from jax.experimental.pallas import tpu as pltpu
from jax.sharding import PartitionSpec as P

ITERS = 3
GAIN = 20.0
HALO = 4
LANES = 128
MOMENTS = 2 * ITERS
VMEM_LIMIT = 48 * 1024 * 1024
AXES = {"x_hi": 2, "y": 4, "z": 8, "x_lo": 2, "core": 2}
FOCUS, BAND = ("x_hi", "y"), ("z", "x_lo", "core")


def focus_index():
    return lax.axis_index("x_hi") * lax.axis_size("y") + lax.axis_index("y")


def tree(terms):
    while len(terms) > 1:
        terms = [sum(terms[i + 1 : i + 2], terms[i]) for i in range(0, len(terms), 2)]
    return terms[0]


def centre(z_ref):
    count = z_ref.shape[0]
    places = [z_ref[p] for p in range(count)]
    mean = tree(places) * (1.0 / count)
    return mean, 1.0 / tree([(z - mean) * (z - mean) for z in places])


def encode_kernel(n, z_hbm, planes_hbm, ready, shares, planes, z_ref, sems, z_sem):
    held, rows, cols = planes.shape
    width = cols // n
    high = 2 * held * rows

    def fetch(t):
        part = pl.ds(pl.multiple_of(t * width, width), width)
        return pltpu.make_async_copy(
            planes_hbm.at[:, :, part], planes.at[:, :, part], sems.at[t]
        )

    fetch_z = pltpu.make_async_copy(z_hbm, z_ref, z_sem)
    fetch_z.start()
    for t in range(n):
        fetch(t).start()
    fetch_z.wait()
    mean, norm = centre(z_ref)
    for p in range(z_ref.shape[0]):
        shares[p : p + 1, :] = jnp.full((1, LANES), (z_ref[p] - mean) * (norm * GAIN))

    lane = lax.broadcasted_iota(jnp.int32, (rows, LANES), 1)
    low = lane < LANES // 2

    def tile(t, carry):
        @pl.when(t < n - 1)
        def _():
            fetch(t + 1).wait()

        for i in range(width // (2 * LANES)):
            part = pl.ds(pl.multiple_of(t * width + i * 2 * LANES, 2 * LANES), 2 * LANES)
            values = [planes[k, :, part].astype(jnp.float32) for k in range(held)]
            values = [v[:, :LANES] for v in values] + [v[:, LANES:] for v in values]
            values = jnp.concatenate(values, axis=0).astype(jnp.bfloat16)
            ready[t, i * high : (i + 1) * high, :] = values
        right = pl.ds(pl.multiple_of(jnp.minimum((t + 1) * width, cols - LANES), LANES), LANES)
        left = pl.ds(pl.multiple_of(jnp.maximum(t * width - LANES, 0), LANES), LANES)
        inside = jnp.where(low, jnp.where(t < n - 1, 1, 0), jnp.where(t > 0, 1, 0)) > 0
        values = [
            jnp.where(
                low, planes[k, :, right].astype(jnp.float32), planes[k, :, left].astype(jnp.float32)
            )
            for k in range(held)
        ]
        values = pack(jnp.concatenate([jnp.where(inside, v, 0.0) for v in values], axis=0))
        values = jnp.concatenate([values, jnp.zeros_like(values)], axis=0)
        ready[t, width // (2 * LANES) * high :, :] = values.astype(jnp.bfloat16)
        return carry

    fetch(0).wait()
    lax.fori_loop(0, n, tile, 0)


def pack(side):
    lane = lax.broadcasted_iota(jnp.int32, (8, LANES), 1) // (2 * HALO)
    out = None
    for g in range(side.shape[0] // 8):
        group = pltpu.roll(side[8 * g : 8 * g + 8], HALO + 2 * HALO * g, 1)
        out = group if out is None else jnp.where(lane == g, group, out)
    return out


def unpack(packed, rows):
    groups = [
        pltpu.roll(packed, LANES - HALO - 2 * HALO * g, 1) for g in range(rows // 8)
    ]
    return jnp.concatenate(groups, axis=0)


def encode(planes, focus_z, n):
    held, rows, cols = planes.shape
    anywhere = pl.BlockSpec(memory_space=pl.ANY)
    height = cols // n // LANES * held * rows + 16
    whole = pl.BlockSpec(memory_space=pltpu.VMEM)
    return pl.pallas_call(
        functools.partial(encode_kernel, n),
        out_shape=(
            jax.ShapeDtypeStruct((n, height, LANES), jnp.bfloat16),
            jax.ShapeDtypeStruct((n * held, LANES), jnp.float32),
        ),
        in_specs=[anywhere, anywhere],
        out_specs=(whole, whole),
        scratch_shapes=[
            pltpu.VMEM(planes.shape, planes.dtype),
            pltpu.SMEM(focus_z.shape, jnp.float32),
            pltpu.SemaphoreType.DMA((n,)),
            pltpu.SemaphoreType.DMA,
        ],
        compiler_params=pltpu.CompilerParams(vmem_limit_bytes=VMEM_LIMIT),
        name="encode",
    )(
        pltpu.with_memory_space_constraint(focus_z, pltpu.HBM),
        pltpu.with_memory_space_constraint(planes, pltpu.HBM),
    )


def decode_kernel(count, shares_ref, got_ref, intensity_ref, rhs_ref, far_ref, near_ref):
    n = got_ref.shape[0]
    rows, wide = intensity_ref.shape
    held = count // n
    high = 2 * held * rows
    weights = [shares_ref[p : p + 1, :] for p in range(count)]
    pairs = wide // (2 * LANES)

    def pair(i, carry):
        start = pl.multiple_of(i * high, 16)
        total, slope = [None, None], [None, None]
        for f in range(n):
            got = got_ref[f, pl.ds(start, high), :].astype(jnp.float32)
            for half in range(2):
                for k in range(held):
                    at = (half * held + k) * rows
                    value = got[at : at + rows]
                    lean = value * weights[f * held + k]
                    first = total[half] is None
                    total[half] = value if first else total[half] + value
                    slope[half] = lean if first else slope[half] + lean
        for half in range(2):
            at = pl.ds(pl.multiple_of((2 * i + half) * LANES, LANES), LANES)
            intensity_ref[:, at] = total[half] * (1.0 / count)
            rhs_ref[:, at] = slope[half]
        return carry

    lax.fori_loop(0, pairs, pair, 0)
    plane = lax.broadcasted_iota(jnp.int32, (1, LANES), 1) // (2 * HALO) // (rows // 8)
    total = slope = None
    for f in range(n):
        value = got_ref[f, pairs * high :, :].astype(jnp.float32)[:8]
        weight = weights[f * held]
        for k in range(1, held):
            weight = jnp.where(plane == k, weights[f * held + k], weight)
        lean = value * weight
        total = value if total is None else total + value
        slope = lean if slope is None else slope + lean
    total, slope = unpack(total, held * rows), unpack(slope, held * rows)
    side = pl.ds(wide - LANES, LANES)
    intensity_ref[:, side] = sum(
        (total[k * rows : (k + 1) * rows] for k in range(1, held)), total[:rows]
    ) * (1.0 / count)
    rhs_ref[:, side] = sum(
        (slope[k * rows : (k + 1) * rows] for k in range(1, held)), slope[:rows]
    )
    up = jnp.concatenate([intensity_ref[:8][:HALO], rhs_ref[:8][:HALO]], axis=0)
    down = jnp.concatenate([intensity_ref[rows - 8 :][HALO:], rhs_ref[rows - 8 :][HALO:]], axis=0)
    even = lax.axis_index("core") == 0
    near_ref[...] = jnp.where(even, down, up)
    far_ref[...] = jnp.where(even, up, down)


def decode(got, shares, count, rows, width):
    whole = pl.BlockSpec(memory_space=pltpu.VMEM)
    tile = jax.ShapeDtypeStruct((rows, width + LANES), jnp.float32)
    edge = jax.ShapeDtypeStruct((2 * HALO, width + LANES), jnp.float32)
    return pl.pallas_call(
        functools.partial(decode_kernel, count),
        out_shape=(tile, tile, edge, edge),
        in_specs=[whole, whole],
        out_specs=(whole, whole, whole, whole),
        compiler_params=pltpu.CompilerParams(vmem_limit_bytes=VMEM_LIMIT),
        name="decode",
    )(shares, got)


def krylov_kernel(width, intensity_ref, rhs_ref, far_ref, near_ref, *out_refs):
    diag_ref, *v_refs, sums_ref = out_refs
    rows = intensity_ref.shape[0]
    core = lax.axis_index("core")
    chip = lax.axis_index("z") * lax.axis_size("x_lo") + lax.axis_index("x_lo")
    top = (core == 0) & (chip == 0)
    bottom = (core == 1) & (chip == lax.axis_size("z") * lax.axis_size("x_lo") - 1)
    near, far = near_ref[...], jnp.where(top | bottom, 0.0, far_ref[...])
    above, below = jnp.where(core == 0, far, near), jnp.where(core == 0, near, far)
    intensity = jnp.concatenate([intensity_ref[...], below[:HALO], above[:HALO]], axis=0)
    rhs = jnp.concatenate([rhs_ref[...], below[HALO:], above[HALO:]], axis=0)
    high, wide = intensity.shape

    def after(x, axis):
        return pltpu.roll(x, x.shape[axis] - 1, axis)

    def before(x, axis):
        return pltpu.roll(x, 1, axis)

    south = 0.5 * (intensity + after(intensity, 0))
    east = 0.5 * (intensity + after(intensity, 1))
    diag = south + before(south, 0) + east + before(east, 1)
    inverse = jnp.where(intensity > 0.0, 1.0 / diag, 0.0)
    v = rhs * inverse
    diag_ref[...] = diag[:rows, :width]
    vectors = [v[:rows, :width]]
    for step in range(ITERS):
        beside = south * after(v, 0) + before(south * v, 0)
        beside = beside + east * after(v, 1) + before(east * v, 1)
        v = v - beside * inverse
        vectors.append(v[:rows, :width])
    for ref, vector in zip(v_refs, vectors):
        ref[...] = vector
    lane = lax.broadcasted_iota(jnp.int32, (1, LANES), 1)
    weighted = [diag[:rows, :width] * vector for vector in vectors[:ITERS]]
    sums = jnp.zeros((1, LANES), jnp.float32)
    for k in range(MOMENTS):
        moment = jnp.sum(weighted[k // 2] * vectors[k - k // 2], axis=0, keepdims=True)
        moment = jnp.sum(moment, axis=1, keepdims=True)
        sums = sums + jnp.where(lane == k, moment, 0.0)
    sums_ref[...] = jnp.broadcast_to(sums, sums_ref.shape)


def krylov(intensity, rhs, far, near, width, copies):
    rows = intensity.shape[0]
    whole = pl.BlockSpec(memory_space=pltpu.VMEM)
    tile = jax.ShapeDtypeStruct((rows, width), jnp.float32)
    return pl.pallas_call(
        functools.partial(krylov_kernel, width),
        out_shape=(tile,) * (ITERS + 2) + (jax.ShapeDtypeStruct((copies, LANES), jnp.float32),),
        in_specs=[whole] * 4,
        out_specs=(whole,) * (ITERS + 3),
        compiler_params=pltpu.CompilerParams(vmem_limit_bytes=VMEM_LIMIT),
        name="krylov",
    )(intensity, rhs, far, near)


def form(left, right, moments):
    terms = [(a * b) * moments[i + j] for i, a in enumerate(left) for j, b in enumerate(right)]
    return tree(terms)


def coefficients(moments):
    one = jnp.ones_like(moments[0])
    zero = jnp.zeros_like(one)
    direction, pre, phase = [one], [one], [zero] * ITERS
    rz = moments[0]
    for step in range(ITERS):
        alpha = rz / form(direction, direction, moments[1:])
        phase = [c + alpha * d for c, d in zip(phase, direction + [zero] * ITERS)]
        pre = [c - alpha * d for c, d in zip(pre + [zero], [zero] + direction)]
        if step + 1 < ITERS:
            new = form(pre, pre, moments)
            ratio = new / rz
            direction = [c + ratio * d for c, d in zip(pre, direction + [zero])]
            rz = new
    return phase, pre


def finish_kernel(sums_ref, diag_ref, *refs):
    v_refs, (phase_ref, residual_ref) = refs[:-2], refs[-2:]
    sums = jnp.sum(sums_ref[...], axis=0, keepdims=True)
    phase, pre = coefficients([sums[:, k : k + 1] for k in range(MOMENTS)])
    vectors = [ref[...] for ref in v_refs]
    out = phase[0] * vectors[0]
    for c, v in zip(phase[1:], vectors[1:]):
        out = out + c * v
    phase_ref[...] = out
    out = pre[0] * vectors[0]
    for c, v in zip(pre[1:], vectors[1:]):
        out = out + c * v
    residual_ref[...] = diag_ref[...] * out


def finish(sums, diag, vectors):
    whole = pl.BlockSpec(memory_space=pltpu.VMEM)
    tile = jax.ShapeDtypeStruct(diag.shape, jnp.float32)
    return pl.pallas_call(
        finish_kernel,
        out_shape=(tile, tile),
        in_specs=[whole] * (2 + len(vectors)),
        out_specs=(whole, whole),
        compiler_params=pltpu.CompilerParams(vmem_limit_bytes=VMEM_LIMIT),
        name="finish",
    )(sums, diag, *vectors)


def body(planes, focus_z):
    focus, band = lax.axis_size(FOCUS), lax.axis_size(BAND)
    rows, width = planes.shape[1], planes.shape[2] // focus
    sent, shares = encode(planes, focus_z, focus)
    got = lax.all_to_all(sent, FOCUS, 0, 0, tiled=True)
    intensity, rhs, far, near = decode(got, shares, focus_z.shape[0], rows, width)
    far = lax.ppermute(far, BAND, [(i, (i + 2 * (i % 2) - 1) % band) for i in range(band)])
    near = lax.ppermute(near, "core", [(0, 1), (1, 0)])
    everyone = FOCUS + BAND
    diag, *vectors, sums = krylov(intensity, rhs, far, near, width, focus * band)
    sums = lax.all_to_all(sums, everyone, 0, 0, tiled=True)
    return finish(sums, diag, vectors)


def solution(mesh):
    parts = jax.sharding.Mesh(mesh.devices.reshape(tuple(AXES.values())), tuple(AXES))
    return jax.shard_map(
        body,
        mesh=parts,
        in_specs=(P(FOCUS, BAND, None), P()),
        out_specs=(P(BAND, FOCUS), P(BAND, FOCUS)),
        check_vma=False,
    )
```

```python
import functools

import jax
import jax.numpy as jnp
import numpy as np
from jax import lax
from jax.experimental import pallas as pl
from jax.experimental.pallas import tpu as pltpu
from jax.sharding import PartitionSpec as P

ITERS = 3
GAIN = 20.0
HALO = 4
LANES = 128
MOMENTS = 2 * ITERS
VMEM_LIMIT = 48 * 1024 * 1024
AXES = {"x_hi": 2, "y": 4, "z": 8, "x_lo": 2, "core": 2}
FOCUS, BAND = ("x_hi", "y"), ("z", "x_lo", "core")


def focus_index():
    return lax.axis_index("x_hi") * lax.axis_size("y") + lax.axis_index("y")


def tree(terms):
    while len(terms) > 1:
        terms = [sum(terms[i + 1 : i + 2], terms[i]) for i in range(0, len(terms), 2)]
    return terms[0]


def centre(z_ref):
    count = z_ref.shape[0]
    places = [z_ref[p] for p in range(count)]
    mean = tree(places) * (1.0 / count)
    return mean, 1.0 / tree([(z - mean) * (z - mean) for z in places])


def encode_kernel(n, z_hbm, planes_hbm, ready, shares, planes, z_ref, sems, z_sem):
    held, rows, cols = planes.shape
    width = cols // n
    high = 2 * held * rows

    def fetch(t):
        part = pl.ds(pl.multiple_of(t * width, width), width)
        return pltpu.make_async_copy(
            planes_hbm.at[:, :, part], planes.at[:, :, part], sems.at[t]
        )

    fetch_z = pltpu.make_async_copy(z_hbm, z_ref, z_sem)
    fetch_z.start()
    for t in range(n):
        fetch(t).start()
    fetch_z.wait()
    mean, norm = centre(z_ref)
    for p in range(z_ref.shape[0]):
        shares[p : p + 1, :] = jnp.full((1, LANES), (z_ref[p] - mean) * (norm * GAIN))

    lane = lax.broadcasted_iota(jnp.int32, (rows, LANES), 1)
    low = lane < LANES // 2

    def tile(t, carry):
        @pl.when(t < n - 1)
        def _():
            fetch(t + 1).wait()

        for i in range(width // (2 * LANES)):
            part = pl.ds(pl.multiple_of(t * width + i * 2 * LANES, 2 * LANES), 2 * LANES)
            values = [planes[k, :, part].astype(jnp.float32) for k in range(held)]
            values = [v[:, :LANES] for v in values] + [v[:, LANES:] for v in values]
            values = jnp.concatenate(values, axis=0).astype(jnp.bfloat16)
            ready[t, i * high : (i + 1) * high, :] = values
        right = pl.ds(pl.multiple_of(jnp.minimum((t + 1) * width, cols - LANES), LANES), LANES)
        left = pl.ds(pl.multiple_of(jnp.maximum(t * width - LANES, 0), LANES), LANES)
        inside = jnp.where(low, jnp.where(t < n - 1, 1, 0), jnp.where(t > 0, 1, 0)) > 0
        values = [
            jnp.where(
                low, planes[k, :, right].astype(jnp.float32), planes[k, :, left].astype(jnp.float32)
            )
            for k in range(held)
        ]
        values = pack(jnp.concatenate([jnp.where(inside, v, 0.0) for v in values], axis=0))
        values = jnp.concatenate([values, jnp.zeros_like(values)], axis=0)
        ready[t, width // (2 * LANES) * high :, :] = values.astype(jnp.bfloat16)
        return carry

    fetch(0).wait()
    lax.fori_loop(0, n, tile, 0)


def pack(side):
    lane = lax.broadcasted_iota(jnp.int32, (8, LANES), 1) // (2 * HALO)
    out = None
    for g in range(side.shape[0] // 8):
        group = pltpu.roll(side[8 * g : 8 * g + 8], HALO + 2 * HALO * g, 1)
        out = group if out is None else jnp.where(lane == g, group, out)
    return out


def unpack(packed, rows):
    groups = [
        pltpu.roll(packed, LANES - HALO - 2 * HALO * g, 1) for g in range(rows // 8)
    ]
    return jnp.concatenate(groups, axis=0)


def encode(planes, focus_z, n):
    held, rows, cols = planes.shape
    anywhere = pl.BlockSpec(memory_space=pl.ANY)
    height = cols // n // LANES * held * rows + 16
    whole = pl.BlockSpec(memory_space=pltpu.VMEM)
    return pl.pallas_call(
        functools.partial(encode_kernel, n),
        out_shape=(
            jax.ShapeDtypeStruct((n, height, LANES), jnp.bfloat16),
            jax.ShapeDtypeStruct((n * held, LANES), jnp.float32),
        ),
        in_specs=[anywhere, anywhere],
        out_specs=(whole, whole),
        scratch_shapes=[
            pltpu.VMEM(planes.shape, planes.dtype),
            pltpu.SMEM(focus_z.shape, jnp.float32),
            pltpu.SemaphoreType.DMA((n,)),
            pltpu.SemaphoreType.DMA,
        ],
        compiler_params=pltpu.CompilerParams(vmem_limit_bytes=VMEM_LIMIT),
        name="encode",
    )(
        pltpu.with_memory_space_constraint(focus_z, pltpu.HBM),
        pltpu.with_memory_space_constraint(planes, pltpu.HBM),
    )


def decode_kernel(count, shares_ref, got_ref, intensity_ref, rhs_ref, far_ref, near_ref):
    n = got_ref.shape[0]
    rows, wide = intensity_ref.shape
    held = count // n
    high = 2 * held * rows
    weights = [shares_ref[p : p + 1, :] for p in range(count)]
    pairs = wide // (2 * LANES)

    def pair(i, carry):
        start = pl.multiple_of(i * high, 16)
        total, slope = [None, None], [None, None]
        for f in range(n):
            got = got_ref[f, pl.ds(start, high), :].astype(jnp.float32)
            for half in range(2):
                for k in range(held):
                    at = (half * held + k) * rows
                    value = got[at : at + rows]
                    lean = value * weights[f * held + k]
                    first = total[half] is None
                    total[half] = value if first else total[half] + value
                    slope[half] = lean if first else slope[half] + lean
        for half in range(2):
            at = pl.ds(pl.multiple_of((2 * i + half) * LANES, LANES), LANES)
            intensity_ref[:, at] = total[half] * (1.0 / count)
            rhs_ref[:, at] = slope[half]
        return carry

    lax.fori_loop(0, pairs, pair, 0)
    plane = lax.broadcasted_iota(jnp.int32, (1, LANES), 1) // (2 * HALO) // (rows // 8)
    total = slope = None
    for f in range(n):
        value = got_ref[f, pairs * high :, :].astype(jnp.float32)[:8]
        weight = weights[f * held]
        for k in range(1, held):
            weight = jnp.where(plane == k, weights[f * held + k], weight)
        lean = value * weight
        total = value if total is None else total + value
        slope = lean if slope is None else slope + lean
    total, slope = unpack(total, held * rows), unpack(slope, held * rows)
    side = pl.ds(wide - LANES, LANES)
    intensity_ref[:, side] = sum(
        (total[k * rows : (k + 1) * rows] for k in range(1, held)), total[:rows]
    ) * (1.0 / count)
    rhs_ref[:, side] = sum(
        (slope[k * rows : (k + 1) * rows] for k in range(1, held)), slope[:rows]
    )
    up = jnp.concatenate([intensity_ref[:8][:HALO], rhs_ref[:8][:HALO]], axis=0)
    down = jnp.concatenate([intensity_ref[rows - 8 :][HALO:], rhs_ref[rows - 8 :][HALO:]], axis=0)
    even = lax.axis_index("core") == 0
    near_ref[...] = jnp.where(even, down, up)
    far_ref[...] = jnp.where(even, up, down)


def decode(got, shares, count, rows, width):
    whole = pl.BlockSpec(memory_space=pltpu.VMEM)
    tile = jax.ShapeDtypeStruct((rows, width + LANES), jnp.float32)
    edge = jax.ShapeDtypeStruct((2 * HALO, width + LANES), jnp.float32)
    return pl.pallas_call(
        functools.partial(decode_kernel, count),
        out_shape=(tile, tile, edge, edge),
        in_specs=[whole, whole],
        out_specs=(whole, whole, whole, whole),
        compiler_params=pltpu.CompilerParams(vmem_limit_bytes=VMEM_LIMIT),
        name="decode",
    )(shares, got)


def krylov_kernel(width, intensity_ref, rhs_ref, far_ref, near_ref, *out_refs):
    diag_ref, *v_refs, sums_ref = out_refs
    rows = intensity_ref.shape[0]
    core = lax.axis_index("core")
    chip = lax.axis_index("z") * lax.axis_size("x_lo") + lax.axis_index("x_lo")
    top = (core == 0) & (chip == 0)
    bottom = (core == 1) & (chip == lax.axis_size("z") * lax.axis_size("x_lo") - 1)
    near, far = near_ref[...], jnp.where(top | bottom, 0.0, far_ref[...])
    above, below = jnp.where(core == 0, far, near), jnp.where(core == 0, near, far)
    intensity = jnp.concatenate([intensity_ref[...], below[:HALO], above[:HALO]], axis=0)
    rhs = jnp.concatenate([rhs_ref[...], below[HALO:], above[HALO:]], axis=0)
    high, wide = intensity.shape

    def after(x, axis):
        return pltpu.roll(x, x.shape[axis] - 1, axis)

    def before(x, axis):
        return pltpu.roll(x, 1, axis)

    south = 0.5 * (intensity + after(intensity, 0))
    east = 0.5 * (intensity + after(intensity, 1))
    diag = south + before(south, 0) + east + before(east, 1)
    inverse = jnp.where(intensity > 0.0, 1.0 / diag, 0.0)
    first = rhs * inverse
    diag_ref[...] = diag[:rows, :width]
    v_refs[0][...] = first[:rows, :width]
    own = diag[:rows, :width]
    lane = lax.broadcasted_iota(jnp.int32, (1, LANES), 1)
    sums = jnp.zeros((1, LANES), jnp.float32)
    for basis, sign in enumerate((-1.0, 1.0)):
        v, vectors = first, [first[:rows, :width]]
        for step in range(ITERS):
            beside = south * after(v, 0) + before(south * v, 0)
            beside = beside + east * after(v, 1) + before(east * v, 1)
            v = v + sign * (beside * inverse)
            vectors.append(v[:rows, :width])
            v_refs[1 + basis * ITERS + step][...] = vectors[-1]
        weighted = [own * vector for vector in vectors[:ITERS]]
        for k in range(MOMENTS):
            moment = jnp.sum(weighted[k // 2] * vectors[k - k // 2], axis=0, keepdims=True)
            moment = jnp.sum(moment, axis=1, keepdims=True)
            sums = sums + jnp.where(lane == basis * MOMENTS + k, moment, 0.0)
    sums_ref[...] = jnp.broadcast_to(sums, sums_ref.shape)


def krylov(intensity, rhs, far, near, width, copies):
    rows = intensity.shape[0]
    whole = pl.BlockSpec(memory_space=pltpu.VMEM)
    tile = jax.ShapeDtypeStruct((rows, width), jnp.float32)
    return pl.pallas_call(
        functools.partial(krylov_kernel, width),
        out_shape=(tile,) * (2 * ITERS + 2) + (jax.ShapeDtypeStruct((copies, LANES), jnp.float32),),
        in_specs=[whole] * 4,
        out_specs=(whole,) * (2 * ITERS + 3),
        compiler_params=pltpu.CompilerParams(vmem_limit_bytes=VMEM_LIMIT),
        name="krylov",
    )(intensity, rhs, far, near)


def form(left, right, moments):
    terms = [(a * b) * moments[i + j] for i, a in enumerate(left) for j, b in enumerate(right)]
    return tree(terms)


def coefficients(moments, stay, move):
    one = jnp.ones_like(moments[0])
    zero = jnp.zeros_like(one)
    direction, pre, phase = [one], [one], [zero] * ITERS
    rz = moments[0]
    for step in range(ITERS):
        image = [stay * a + move * b for a, b in zip(direction + [zero], [zero] + direction)]
        alpha = rz / form(direction, image, moments)
        phase = [c + alpha * d for c, d in zip(phase, direction + [zero] * ITERS)]
        pre = [c - alpha * d for c, d in zip(pre + [zero], image)]
        if step + 1 < ITERS:
            new = form(pre, pre, moments)
            ratio = new / rz
            direction = [c + ratio * d for c, d in zip(pre, direction + [zero])]
            rz = new
    return phase, pre


def finish_kernel(sums_ref, diag_ref, *refs):
    v_refs, (phase_ref, residual_ref) = refs[:-2], refs[-2:]
    sums = jnp.sum(sums_ref[...], axis=0, keepdims=True)
    one_each = [sums[:, k : k + 1] for k in range(2 * MOMENTS)]
    rough = one_each[1] > one_each[0]
    moments = [jnp.where(rough, b, a) for a, b in zip(one_each[:MOMENTS], one_each[MOMENTS:])]
    phase, pre = coefficients(
        moments, jnp.where(rough, 2.0, 0.0), jnp.where(rough, -1.0, 1.0)
    )
    vectors = [v_refs[0][...]]
    for a, b in zip(v_refs[1 : ITERS + 1], v_refs[ITERS + 1 :]):
        vectors.append(jnp.where(rough, b[...], a[...]))
    out = phase[0] * vectors[0]
    for c, v in zip(phase[1:], vectors[1:]):
        out = out + c * v
    phase_ref[...] = out
    out = pre[0] * vectors[0]
    for c, v in zip(pre[1:], vectors[1:]):
        out = out + c * v
    residual_ref[...] = diag_ref[...] * out


def finish(sums, diag, vectors):
    whole = pl.BlockSpec(memory_space=pltpu.VMEM)
    tile = jax.ShapeDtypeStruct(diag.shape, jnp.float32)
    return pl.pallas_call(
        finish_kernel,
        out_shape=(tile, tile),
        in_specs=[whole] * (2 + len(vectors)),
        out_specs=(whole, whole),
        compiler_params=pltpu.CompilerParams(vmem_limit_bytes=VMEM_LIMIT),
        name="finish",
    )(sums, diag, *vectors)


def body(planes, focus_z):
    focus, band = lax.axis_size(FOCUS), lax.axis_size(BAND)
    rows, width = planes.shape[1], planes.shape[2] // focus
    sent, shares = encode(planes, focus_z, focus)
    got = lax.all_to_all(sent, FOCUS, 0, 0, tiled=True)
    intensity, rhs, far, near = decode(got, shares, focus_z.shape[0], rows, width)
    far = lax.ppermute(far, BAND, [(i, (i + 2 * (i % 2) - 1) % band) for i in range(band)])
    near = lax.ppermute(near, "core", [(0, 1), (1, 0)])
    everyone = FOCUS + BAND
    diag, *vectors, sums = krylov(intensity, rhs, far, near, width, focus * band)
    sums = lax.all_to_all(sums, everyone, 0, 0, tiled=True)
    return finish(sums, diag, vectors)


def solution(mesh):
    parts = jax.sharding.Mesh(mesh.devices.reshape(tuple(AXES.values())), tuple(AXES))
    return jax.shard_map(
        body,
        mesh=parts,
        in_specs=(P(FOCUS, BAND, None), P()),
        out_specs=(P(BAND, FOCUS), P(BAND, FOCUS)),
        check_vma=False,
    )
```

```python
import functools

import jax
import jax.numpy as jnp
import numpy as np
from jax import lax
from jax.experimental import pallas as pl
from jax.experimental.pallas import tpu as pltpu
from jax.sharding import PartitionSpec as P

ITERS = 3
GAIN = 20.0
HALO = 4
LANES = 128
MOMENTS = 2 * ITERS
VMEM_LIMIT = 48 * 1024 * 1024
AXES = {"x_hi": 2, "y": 4, "z": 8, "x_lo": 2, "core": 2}
FOCUS, BAND = ("x_hi", "y"), ("z", "x_lo", "core")


def focus_index():
    return lax.axis_index("x_hi") * lax.axis_size("y") + lax.axis_index("y")


def tree(terms):
    while len(terms) > 1:
        terms = [sum(terms[i + 1 : i + 2], terms[i]) for i in range(0, len(terms), 2)]
    return terms[0]


def centre(z_ref):
    count = z_ref.shape[0]
    places = [z_ref[p] for p in range(count)]
    mean = tree(places) * (1.0 / count)
    return mean, 1.0 / tree([(z - mean) * (z - mean) for z in places])


def encode_kernel(n, z_hbm, planes_hbm, ready, shares, planes, z_ref, sems, z_sem):
    held, rows, cols = planes.shape
    width = cols // n
    high = 2 * held * rows

    def fetch(t):
        part = pl.ds(pl.multiple_of(t * width, width), width)
        return pltpu.make_async_copy(
            planes_hbm.at[:, :, part], planes.at[:, :, part], sems.at[t]
        )

    fetch_z = pltpu.make_async_copy(z_hbm, z_ref, z_sem)
    fetch_z.start()
    for t in range(n):
        fetch(t).start()
    fetch_z.wait()
    mean, norm = centre(z_ref)
    for p in range(z_ref.shape[0]):
        shares[p : p + 1, :] = jnp.full((1, LANES), (z_ref[p] - mean) * (norm * GAIN))

    lane = lax.broadcasted_iota(jnp.int32, (rows, LANES), 1)
    low = lane < LANES // 2

    def tile(t, carry):
        @pl.when(t < n - 1)
        def _():
            fetch(t + 1).wait()

        for i in range(width // (2 * LANES)):
            part = pl.ds(pl.multiple_of(t * width + i * 2 * LANES, 2 * LANES), 2 * LANES)
            values = [planes[k, :, part].astype(jnp.float32) for k in range(held)]
            values = [v[:, :LANES] for v in values] + [v[:, LANES:] for v in values]
            values = jnp.concatenate(values, axis=0).astype(jnp.bfloat16)
            ready[t, i * high : (i + 1) * high, :] = values
        right = pl.ds(pl.multiple_of(jnp.minimum((t + 1) * width, cols - LANES), LANES), LANES)
        left = pl.ds(pl.multiple_of(jnp.maximum(t * width - LANES, 0), LANES), LANES)
        inside = jnp.where(low, jnp.where(t < n - 1, 1, 0), jnp.where(t > 0, 1, 0)) > 0
        values = [
            jnp.where(
                low, planes[k, :, right].astype(jnp.float32), planes[k, :, left].astype(jnp.float32)
            )
            for k in range(held)
        ]
        values = pack(jnp.concatenate([jnp.where(inside, v, 0.0) for v in values], axis=0))
        values = jnp.concatenate([values, jnp.zeros_like(values)], axis=0)
        ready[t, width // (2 * LANES) * high :, :] = values.astype(jnp.bfloat16)
        return carry

    fetch(0).wait()
    lax.fori_loop(0, n, tile, 0)


def pack(side):
    lane = lax.broadcasted_iota(jnp.int32, (8, LANES), 1) // (2 * HALO)
    out = None
    for g in range(side.shape[0] // 8):
        group = pltpu.roll(side[8 * g : 8 * g + 8], HALO + 2 * HALO * g, 1)
        out = group if out is None else jnp.where(lane == g, group, out)
    return out


def unpack(packed, rows):
    groups = [
        pltpu.roll(packed, LANES - HALO - 2 * HALO * g, 1) for g in range(rows // 8)
    ]
    return jnp.concatenate(groups, axis=0)


def encode(planes, focus_z, n):
    held, rows, cols = planes.shape
    anywhere = pl.BlockSpec(memory_space=pl.ANY)
    height = cols // n // LANES * held * rows + 16
    whole = pl.BlockSpec(memory_space=pltpu.VMEM)
    return pl.pallas_call(
        functools.partial(encode_kernel, n),
        out_shape=(
            jax.ShapeDtypeStruct((n, height, LANES), jnp.bfloat16),
            jax.ShapeDtypeStruct((n * held, LANES), jnp.float32),
        ),
        in_specs=[anywhere, anywhere],
        out_specs=(whole, whole),
        scratch_shapes=[
            pltpu.VMEM(planes.shape, planes.dtype),
            pltpu.SMEM(focus_z.shape, jnp.float32),
            pltpu.SemaphoreType.DMA((n,)),
            pltpu.SemaphoreType.DMA,
        ],
        compiler_params=pltpu.CompilerParams(vmem_limit_bytes=VMEM_LIMIT),
        name="encode",
    )(
        pltpu.with_memory_space_constraint(focus_z, pltpu.HBM),
        pltpu.with_memory_space_constraint(planes, pltpu.HBM),
    )


def decode_kernel(count, shares_ref, got_ref, intensity_ref, rhs_ref, far_ref, near_ref):
    n = got_ref.shape[0]
    rows, wide = intensity_ref.shape
    held = count // n
    high = 2 * held * rows
    weights = [shares_ref[p : p + 1, :] for p in range(count)]
    pairs = wide // (2 * LANES)

    def pair(i, carry):
        start = pl.multiple_of(i * high, 16)
        total, slope = [None, None], [None, None]
        for f in range(n):
            got = got_ref[f, pl.ds(start, high), :].astype(jnp.float32)
            for half in range(2):
                for k in range(held):
                    at = (half * held + k) * rows
                    value = got[at : at + rows]
                    lean = value * weights[f * held + k]
                    first = total[half] is None
                    total[half] = value if first else total[half] + value
                    slope[half] = lean if first else slope[half] + lean
        for half in range(2):
            at = pl.ds(pl.multiple_of((2 * i + half) * LANES, LANES), LANES)
            intensity_ref[:, at] = total[half] * (1.0 / count)
            rhs_ref[:, at] = slope[half]
        return carry

    lax.fori_loop(0, pairs, pair, 0)
    plane = lax.broadcasted_iota(jnp.int32, (1, LANES), 1) // (2 * HALO) // (rows // 8)
    total = slope = None
    for f in range(n):
        value = got_ref[f, pairs * high :, :].astype(jnp.float32)[:8]
        weight = weights[f * held]
        for k in range(1, held):
            weight = jnp.where(plane == k, weights[f * held + k], weight)
        lean = value * weight
        total = value if total is None else total + value
        slope = lean if slope is None else slope + lean
    total, slope = unpack(total, held * rows), unpack(slope, held * rows)
    side = pl.ds(wide - LANES, LANES)
    intensity_ref[:, side] = sum(
        (total[k * rows : (k + 1) * rows] for k in range(1, held)), total[:rows]
    ) * (1.0 / count)
    rhs_ref[:, side] = sum(
        (slope[k * rows : (k + 1) * rows] for k in range(1, held)), slope[:rows]
    )
    up = jnp.concatenate([intensity_ref[:8][:HALO], rhs_ref[:8][:HALO]], axis=0)
    down = jnp.concatenate([intensity_ref[rows - 8 :][HALO:], rhs_ref[rows - 8 :][HALO:]], axis=0)
    even = lax.axis_index("core") == 0
    near_ref[...] = jnp.where(even, down, up)
    far_ref[...] = jnp.where(even, up, down)


def decode(got, shares, count, rows, width):
    whole = pl.BlockSpec(memory_space=pltpu.VMEM)
    tile = jax.ShapeDtypeStruct((rows, width + LANES), jnp.float32)
    edge = jax.ShapeDtypeStruct((2 * HALO, width + LANES), jnp.float32)
    return pl.pallas_call(
        functools.partial(decode_kernel, count),
        out_shape=(tile, tile, edge, edge),
        in_specs=[whole, whole],
        out_specs=(whole, whole, whole, whole),
        compiler_params=pltpu.CompilerParams(vmem_limit_bytes=VMEM_LIMIT),
        name="decode",
    )(shares, got)


def krylov_kernel(width, intensity_ref, rhs_ref, far_ref, near_ref, *out_refs):
    diag_ref, *v_refs, sums_ref = out_refs
    rows = intensity_ref.shape[0]
    core = lax.axis_index("core")
    chip = lax.axis_index("z") * lax.axis_size("x_lo") + lax.axis_index("x_lo")
    top = (core == 0) & (chip == 0)
    bottom = (core == 1) & (chip == lax.axis_size("z") * lax.axis_size("x_lo") - 1)
    near, far = near_ref[...], jnp.where(top | bottom, 0.0, far_ref[...])
    above, below = jnp.where(core == 0, far, near), jnp.where(core == 0, near, far)
    intensity = jnp.concatenate([intensity_ref[...], below[:HALO], above[:HALO]], axis=0)
    rhs = jnp.concatenate([rhs_ref[...], below[HALO:], above[HALO:]], axis=0)
    high, wide = intensity.shape

    def after(x, axis):
        return pltpu.roll(x, x.shape[axis] - 1, axis)

    def before(x, axis):
        return pltpu.roll(x, 1, axis)

    south = 0.5 * (intensity + after(intensity, 0))
    east = 0.5 * (intensity + after(intensity, 1))
    diag = south + before(south, 0) + east + before(east, 1)
    inverse = jnp.where(intensity > 0.0, 1.0 / diag, 0.0)
    first = rhs * inverse
    diag_ref[...] = diag[:rows, :width]
    v_refs[0][...] = first[:rows, :width]
    own = diag[:rows, :width]
    parts = []
    for basis, sign in enumerate((-1.0, 1.0)):
        v, vectors = first, [first[:rows, :width]]
        for step in range(ITERS):
            beside = south * after(v, 0) + before(south * v, 0)
            beside = beside + east * after(v, 1) + before(east * v, 1)
            v = v + sign * (beside * inverse)
            vectors.append(v[:rows, :width])
            v_refs[1 + basis * ITERS + step][...] = vectors[-1]
        weighted = [own * vector for vector in vectors[:ITERS]]
        for k in range(MOMENTS):
            part = weighted[k // 2] * vectors[k - k // 2]
            part = sum((part[r : r + 8] for r in range(8, rows, 8)), part[:8])
            part = sum(
                (part[:, c : c + LANES] for c in range(LANES, width, LANES)), part[:, :LANES]
            )
            parts.append(jnp.sum(part, axis=0, keepdims=True))
    sums = jnp.sum(jnp.concatenate(parts, axis=0), axis=1, keepdims=True)
    row = lax.broadcasted_iota(jnp.int32, (2 * MOMENTS, LANES), 0)
    lane = lax.broadcasted_iota(jnp.int32, (2 * MOMENTS, LANES), 1)
    sums = jnp.sum(jnp.where(row == lane, sums, 0.0), axis=0, keepdims=True)
    sums_ref[...] = jnp.broadcast_to(sums, sums_ref.shape)


def krylov(intensity, rhs, far, near, width, copies):
    rows = intensity.shape[0]
    whole = pl.BlockSpec(memory_space=pltpu.VMEM)
    tile = jax.ShapeDtypeStruct((rows, width), jnp.float32)
    return pl.pallas_call(
        functools.partial(krylov_kernel, width),
        out_shape=(tile,) * (2 * ITERS + 2) + (jax.ShapeDtypeStruct((copies, LANES), jnp.float32),),
        in_specs=[whole] * 4,
        out_specs=(whole,) * (2 * ITERS + 3),
        compiler_params=pltpu.CompilerParams(vmem_limit_bytes=VMEM_LIMIT),
        name="krylov",
    )(intensity, rhs, far, near)


def form(left, right, moments):
    terms = [(a * b) * moments[i + j] for i, a in enumerate(left) for j, b in enumerate(right)]
    return tree(terms)


def coefficients(moments, stay, move):
    one = jnp.ones_like(moments[0])
    zero = jnp.zeros_like(one)
    direction, pre, phase = [one], [one], [zero] * ITERS
    rz = moments[0]
    for step in range(ITERS):
        image = [stay * a + move * b for a, b in zip(direction + [zero], [zero] + direction)]
        alpha = rz / form(direction, image, moments)
        phase = [c + alpha * d for c, d in zip(phase, direction + [zero] * ITERS)]
        pre = [c - alpha * d for c, d in zip(pre + [zero], image)]
        if step + 1 < ITERS:
            new = form(pre, pre, moments)
            ratio = new / rz
            direction = [c + ratio * d for c, d in zip(pre, direction + [zero])]
            rz = new
    return phase, pre


def finish_kernel(sums_ref, diag_ref, *refs):
    v_refs, (phase_ref, residual_ref) = refs[:-2], refs[-2:]
    sums = jnp.sum(sums_ref[...], axis=0, keepdims=True)
    one_each = [sums[:, k : k + 1] for k in range(2 * MOMENTS)]
    rough = one_each[1] > one_each[0]
    moments = [jnp.where(rough, b, a) for a, b in zip(one_each[:MOMENTS], one_each[MOMENTS:])]
    phase, pre = coefficients(
        moments, jnp.where(rough, 2.0, 0.0), jnp.where(rough, -1.0, 1.0)
    )
    vectors = [v_refs[0][...]]
    for a, b in zip(v_refs[1 : ITERS + 1], v_refs[ITERS + 1 :]):
        vectors.append(jnp.where(rough, b[...], a[...]))
    out = phase[0] * vectors[0]
    for c, v in zip(phase[1:], vectors[1:]):
        out = out + c * v
    phase_ref[...] = out
    out = pre[0] * vectors[0]
    for c, v in zip(pre[1:], vectors[1:]):
        out = out + c * v
    residual_ref[...] = diag_ref[...] * out


def finish(sums, diag, vectors):
    whole = pl.BlockSpec(memory_space=pltpu.VMEM)
    tile = jax.ShapeDtypeStruct(diag.shape, jnp.float32)
    return pl.pallas_call(
        finish_kernel,
        out_shape=(tile, tile),
        in_specs=[whole] * (2 + len(vectors)),
        out_specs=(whole, whole),
        compiler_params=pltpu.CompilerParams(vmem_limit_bytes=VMEM_LIMIT),
        name="finish",
    )(sums, diag, *vectors)


def body(planes, focus_z):
    focus, band = lax.axis_size(FOCUS), lax.axis_size(BAND)
    rows, width = planes.shape[1], planes.shape[2] // focus
    sent, shares = encode(planes, focus_z, focus)
    got = lax.all_to_all(sent, FOCUS, 0, 0, tiled=True)
    intensity, rhs, far, near = decode(got, shares, focus_z.shape[0], rows, width)
    far = lax.ppermute(far, BAND, [(i, (i + 2 * (i % 2) - 1) % band) for i in range(band)])
    near = lax.ppermute(near, "core", [(0, 1), (1, 0)])
    everyone = FOCUS + BAND
    diag, *vectors, sums = krylov(intensity, rhs, far, near, width, focus * band)
    sums = lax.all_to_all(sums, everyone, 0, 0, tiled=True)
    return finish(sums, diag, vectors)


def solution(mesh):
    parts = jax.sharding.Mesh(mesh.devices.reshape(tuple(AXES.values())), tuple(AXES))
    return jax.shard_map(
        body,
        mesh=parts,
        in_specs=(P(FOCUS, BAND, None), P()),
        out_specs=(P(BAND, FOCUS), P(BAND, FOCUS)),
        check_vma=False,
    )
```
